256 devices in a mesh: clip: 4 (over x), vid: 16 (over z, core), aud: 4 (over y).
Axes of the slice: x: 4, y: 4, z: 8, core: 2. Of those that a mesh axis runs over, the one named last changes fastest.
Arguments:
- video_query: bfloat16 [4, 32768, 1536], P('clip', ('vid', 'aud')), may hold values from -100 to 100
- audio_key: bfloat16 [4, 8192, 1536], P('clip', ('vid', 'aud')), may hold values from -4 to 4
- audio_value: bfloat16 [4, 8192, 1536], P('clip', ('vid', 'aud')), may hold values from -6 to 6
- cross_gate: float32 [1536], replicated, may hold values from 0.5 to 1.5
- grad_out: bfloat16 [4, 32768, 1536], P('clip', ('vid', 'aud')), may hold values from -6 to 6
- pair_blocks: int32 [4, 256, 4], P('clip', ('vid', 'aud')), may hold values from 0 to 63, as said below
- pair_count: int32 [4, 256], P('clip', ('vid', 'aud')), may hold values from 1 to 4
Outputs:
- cross_out: bfloat16 [4, 32768, 1536], P('clip', ('vid', 'aud'))
- query_grad: bfloat16 [4, 32768, 1536], P('clip', ('vid', 'aud'))
- key_grad: bfloat16 [4, 8192, 1536], P('clip', ('vid', 'aud'))
- value_grad: bfloat16 [4, 8192, 1536], P('clip', ('vid', 'aud'))
- gate_grad: float32 [1536], replicated
The draws below stay inside these ranges and needn't reach their ends.
Inputs may be any that keep to these rules, and one draw needn't show every extreme that they name: pair_blocks[c, b, 0] is b // 4, the time-aligned audio block; every entry lies within 2 blocks of it; entries 1 and later of a row are distinct before they are clipped to the clip's blocks.
All inputs are finite; a program needn't handle non-finite values.
Results may differ from the reference program's by a relative error of at most 0.03.
Values may be sent and summed in bfloat16 or wider, within the bound.
No kernel may reach another device: no remote copies, remote signals or barrier semaphores. Data moves between devices by JAX's collectives and lax.ppermute only.
A program may use at most 128 MiB of HBM per device.

```python
import jax
import jax.numpy as jnp
from jax import lax

HEADS = 12
HEAD_DIM = 128
BLOCK = 128
RATIO = 4
REACH = 2
MAXP = 4
CLIPS = 4
ABLK = 64
VBLK = 256
ATOK = 8192
VTOK = 32768
HD = 1536


def shared_keys(key):
    return jnp.clip(jax.random.normal(key, (CLIPS, ATOK, HEADS * HEAD_DIM), jnp.float32), -4.0, 4.0)


def draw_audio_key(key, part):
    base = shared_keys(key)
    return base.astype(jnp.bfloat16)


def draw_video_query(key, part):
    key = jax.random.fold_in(key, 7)
    fresh = jnp.clip(jax.random.normal(key, (CLIPS, VTOK, HEADS * HEAD_DIM), jnp.float32), -4.0, 4.0)
    return fresh.astype(jnp.bfloat16)


def draw_pair_blocks(key, part):
    key = jax.random.fold_in(key, 3)
    centre = jnp.arange(VBLK, dtype=jnp.int32) // RATIO
    width = 2 * REACH
    scores = jax.random.randint(key, (CLIPS, VBLK, width), 0, 1 << 20) * width + jnp.arange(width, dtype=jnp.int32)
    order = jnp.argsort(scores, axis=-1, stable=True)
    candidates = jnp.concatenate([jnp.arange(-REACH, 0, dtype=jnp.int32), jnp.arange(1, REACH + 1, dtype=jnp.int32)])
    offsets = jnp.take(candidates, order[..., :MAXP - 1])
    offsets = jnp.concatenate([jnp.zeros((CLIPS, VBLK, 1), jnp.int32), offsets], axis=-1)
    return jnp.clip(centre[None, :, None] + offsets, 0, ABLK - 1).astype(jnp.int32)


def draw_pair_count(key, part):
    key = jax.random.fold_in(key, 9)
    counts = jax.random.randint(key, (CLIPS, VBLK), 1, MAXP + 1)
    spot = jax.random.randint(jax.random.fold_in(key, 1), (CLIPS, 1), 0, VBLK)
    return jnp.where(jnp.arange(VBLK)[None, :] == spot, MAXP, counts).astype(jnp.int32)


def shard_levels(own_key, dims, shards, low, top_value):
    def one(position, parts):
        heights = jax.random.uniform(jax.random.fold_in(jax.random.fold_in(own_key, 6), position), (parts,), jnp.float32, low / len(shards), top_value / len(shards))
        return jnp.repeat(jnp.exp(heights), dims[position] // parts).reshape((-1,) + (1,) * (len(dims) - position - 1))

    factor_of = one(*shards[0])
    for cut in shards[1:]:
        factor_of = factor_of * one(*cut)
    return factor_of


def scatter_about(own_key, extent, spread, bound, shards=(), kind=jnp.bfloat16):
    gain = shard_levels(own_key, extent, shards, -0.22, 0.18) if shards else 1.0
    entries = jax.random.normal(own_key, extent, jnp.float32) * spread * gain
    return jnp.minimum(jnp.maximum(entries, -bound), bound).astype(kind)


def setup_inputs(seed: int = 0) -> dict:
    arg_keys = jax.random.split(jax.random.key(seed), 8)
    video_query = draw_video_query(jax.random.fold_in(arg_keys[7], 71), 0)
    audio_key = draw_audio_key(jax.random.fold_in(arg_keys[7], 71), 0)
    audio_value = scatter_about(arg_keys[2], (CLIPS, ATOK, HD), 1.0, 6.0, ((0, 4), (1, 64)))
    cross_gate = jnp.clip(jax.random.uniform(arg_keys[3], (HD,), jnp.float32, 0.5, 1.5), 0.5, 1.5)
    grad_out = scatter_about(arg_keys[4], (CLIPS, VTOK, HD), 1.0, 6.0, ((0, 4), (1, 64)))
    pair_blocks = draw_pair_blocks(jax.random.fold_in(arg_keys[7], 71), 0)
    pair_count = draw_pair_count(jax.random.fold_in(arg_keys[7], 71), 0)
    return dict(video_query=video_query, audio_key=audio_key, audio_value=audio_value, cross_gate=cross_gate, grad_out=grad_out, pair_blocks=pair_blocks, pair_count=pair_count)


def reference(video_query, audio_key, audio_value, cross_gate, grad_out, pair_blocks, pair_count):
    scale = HEAD_DIM ** -0.5
    gate = cross_gate.reshape(HEADS, HEAD_DIM)
    outs, qgrads, kgrads, vgrads = [], [], [], []
    gate_sum = jnp.zeros((HEADS, HEAD_DIM), jnp.float32)
    for clip_id in range(CLIPS):
        queries = video_query[clip_id].reshape(VBLK, BLOCK, HEADS, HEAD_DIM)
        upstream = grad_out[clip_id].reshape(VBLK, BLOCK, HEADS, HEAD_DIM)
        key_blocks = audio_key[clip_id].reshape(ABLK, BLOCK, HEADS, HEAD_DIM)
        value_blocks = audio_value[clip_id].reshape(ABLK, BLOCK, HEADS, HEAD_DIM)

        def visit(carry, item):
            key_acc, value_acc, gate_acc = carry
            query_block, up_block, ids, count = item
            keys = jnp.take(key_blocks, ids, axis=0).astype(jnp.float32)
            values = jnp.take(value_blocks, ids, axis=0).astype(jnp.float32)
            qfloat = query_block.astype(jnp.float32)
            scores = jnp.einsum("qhd,mkhd->hqmk", qfloat, keys) * scale
            live = (jnp.arange(MAXP) < count)[None, None, :, None]
            scores = jnp.where(live, scores, -1e30)
            top = jnp.max(scores, axis=(2, 3), keepdims=True)
            expo = jnp.exp(scores - top)
            prob = expo / jnp.sum(expo, axis=(2, 3), keepdims=True)
            prob16 = lax.optimization_barrier(prob.astype(jnp.bfloat16)).astype(jnp.float32)
            attend = jnp.einsum("hqmk,mkhd->qhd", prob16, values)
            out_block = (attend * gate).astype(jnp.bfloat16)
            upfloat = up_block.astype(jnp.float32)
            gate_acc = gate_acc + jnp.sum(attend * upfloat, axis=0)
            dattend = lax.optimization_barrier((upfloat * gate).astype(jnp.bfloat16)).astype(jnp.float32)
            dprob = jnp.einsum("qhd,mkhd->hqmk", dattend, values)
            delta = jnp.transpose(jnp.sum(dattend * attend, axis=-1))[:, :, None, None]
            dscore = lax.optimization_barrier((prob * (dprob - delta)).astype(jnp.bfloat16)).astype(jnp.float32)
            qgrad = (jnp.einsum("hqmk,mkhd->qhd", dscore, keys) * scale).astype(jnp.bfloat16)
            kpart = jnp.einsum("hqmk,qhd->mkhd", dscore, qfloat) * scale
            vpart = jnp.einsum("hqmk,qhd->mkhd", prob16, dattend)
            key_acc = key_acc.at[ids].add(kpart)
            value_acc = value_acc.at[ids].add(vpart)
            return (key_acc, value_acc, gate_acc), (out_block, qgrad)

        start = (jnp.zeros((ABLK, BLOCK, HEADS, HEAD_DIM), jnp.float32),
                 jnp.zeros((ABLK, BLOCK, HEADS, HEAD_DIM), jnp.float32),
                 jnp.zeros((HEADS, HEAD_DIM), jnp.float32))
        (key_acc, value_acc, gate_acc), (out_all, qgrad_all) = lax.scan(
            visit, start, (queries, upstream, pair_blocks[clip_id].astype(jnp.int32), pair_count[clip_id].astype(jnp.int32)))
        gate_sum = gate_sum + gate_acc
        outs.append(out_all.reshape(VTOK, HD))
        qgrads.append(qgrad_all.reshape(VTOK, HD))
        kgrads.append(key_acc.reshape(ATOK, HD).astype(jnp.bfloat16))
        vgrads.append(value_acc.reshape(ATOK, HD).astype(jnp.bfloat16))
    return (jnp.stack(outs), jnp.stack(qgrads), jnp.stack(kgrads), jnp.stack(vgrads), gate_sum.reshape(HD))
```

```python
import math

import jax
import jax.numpy as jnp
from jax import lax
from jax.experimental import pallas as pl
from jax.experimental.pallas import tpu as pltpu
from jax.sharding import PartitionSpec as P

HEADS = 12
HEAD_DIM = 128
BLOCK = 128
REACH = 2
MAXP = 4
WINDOW = 2 * REACH + 1
SCALE = HEAD_DIM**-0.5
LOG2E = math.log2(math.e)
F32 = jnp.float32
BF16 = jnp.bfloat16
TIME = ("vid", "aud")


def nn(a, b):
    return lax.dot_general(a, b, (((1,), (0,)), ((), ())), preferred_element_type=F32)


def nt(a, b):
    return lax.dot_general(a, b, (((1,), (1,)), ((), ())), preferred_element_type=F32)


def tn(a, b):
    return lax.dot_general(a, b, (((0,), (0,)), ((), ())), preferred_element_type=F32)


def weigh(pairs, counts, slot, block):
    times = jnp.int32(0)
    for s in range(MAXP):
        named = pairs[0, block, s] - pairs[0, block, 0] + REACH == slot
        times = times + jnp.where(jnp.logical_and(named, s < counts[0, block]), 1, 0)
    several = jnp.where(times == 2, 1.0, jnp.where(times == 3, math.log2(3.0), 2.0))
    return jnp.where(times == 0, -1e30, jnp.where(times == 1, 0.0, several))


def one_head(queries, upstream, gate, keys, values, bias):
    upf = upstream.astype(F32)
    dattend = (upf * gate).astype(BF16)
    dattend_t = dattend.T
    scores = [nt(k, queries) for k in keys]
    fold = SCALE * LOG2E
    tops = [
        jnp.max(s, axis=0, keepdims=True) * fold + b for s, b in zip(scores, bias)
    ]
    top = tops[0]
    for other in tops[1:]:
        top = jnp.maximum(top, other)
    expo = [jnp.exp2(s * fold + (b - top)) for s, b in zip(scores, bias)]
    total = sum(jnp.sum(e, axis=0, keepdims=True) for e in expo)
    inverse = 1.0 / total
    prob = [e * inverse for e in expo]
    prob16 = [p.astype(BF16) for p in prob]
    attend_t = sum(tn(v, p) for v, p in zip(values, prob16))
    delta = jnp.sum(attend_t * dattend_t.astype(F32), axis=0, keepdims=True)
    attend = attend_t.T
    out = (attend * gate).astype(BF16)
    gate_part = jnp.sum(attend * upf, axis=0, keepdims=True)
    dscore = [
        (p * (nn(v, dattend_t) - delta)).astype(BF16) for p, v in zip(prob, values)
    ]
    qgrad_t = sum(tn(k, d) for k, d in zip(keys, dscore)) * SCALE
    qgrad = qgrad_t.astype(BF16).T
    kparts = [nn(d, queries) * SCALE for d in dscore]
    vparts = [nn(p, dattend) for p in prob16]
    return out, qgrad, gate_part, kparts, vparts


def pair_kernel(
    pairs, counts, q_ref, up_ref, gate_ref,
    k0, v0, kvm1, kvp1, km2, vm2, kp2, vp2,
    out_ref, qgrad_ref, gpart_ref, own_ref, dm1, dp1, dkm2, dvm2, dkp2, dvp2, bias_ref,
):
    @pl.when(pl.program_id(0) == 0)
    def _():
        for slot in range(WINDOW):
            for block in range(4):
                bias_ref[slot : slot + 1, block * BLOCK : (block + 1) * BLOCK] = jnp.full(
                    (1, BLOCK), weigh(pairs, counts, slot, block), F32
                )

    bias = [bias_ref[slot : slot + 1, :] for slot in range(WINDOW)]
    keys = [km2[...], kvm1[0], k0[0], kvp1[0], kp2[...]]
    values = [vm2[...], kvm1[1], v0[0], kvp1[1], vp2[...]]
    out, qgrad, gate_part, kparts, vparts = one_head(
        q_ref[0], up_ref[0], gate_ref[...], keys, values, bias
    )
    out_ref[0] = out
    qgrad_ref[0] = qgrad
    gpart_ref[...] = gate_part
    own_ref[0] = kparts[2]
    own_ref[1] = vparts[2]
    dm1[0] = kparts[1].astype(BF16)
    dm1[1] = vparts[1].astype(BF16)
    dp1[0] = kparts[3].astype(BF16)
    dp1[1] = vparts[3].astype(BF16)
    dkm2[...] = kparts[0].astype(BF16)
    dvm2[...] = vparts[0].astype(BF16)
    dkp2[...] = kparts[4].astype(BF16)
    dvp2[...] = vparts[4].astype(BF16)


def attend_pairs(pairs, counts, queries, upstream, gate, k0, v0, kvm1, kvp1, km2, vm2, kp2, vp2):
    vrows, width = queries.shape[1:]
    smem = pl.BlockSpec(memory_space=pltpu.SMEM)
    video = pl.BlockSpec((1, vrows, HEAD_DIM), lambda h: (0, 0, h))
    own = pl.BlockSpec((1, BLOCK, HEAD_DIM), lambda h: (0, 0, h))
    both = pl.BlockSpec((2, BLOCK, HEAD_DIM), lambda h: (0, 0, h))
    one = pl.BlockSpec((BLOCK, HEAD_DIM), lambda h: (0, h))
    row = pl.BlockSpec((1, HEAD_DIM), lambda h: (0, h))
    shape = jax.ShapeDtypeStruct
    return pl.pallas_call(
        pair_kernel,
        grid=(HEADS,),
        in_specs=[smem, smem, video, video, row, own, own, both, both, one, one, one, one],
        out_specs=[video, video, row, both, both, both, one, one, one, one],
        out_shape=[
            shape((1, vrows, width), BF16),
            shape((1, vrows, width), BF16),
            shape((1, width), F32),
            shape((2, BLOCK, width), F32),
            shape((2, BLOCK, width), BF16),
            shape((2, BLOCK, width), BF16),
        ]
        + [shape((BLOCK, width), BF16)] * 4,
        scratch_shapes=[pltpu.VMEM((8, vrows), F32)],
        compiler_params=pltpu.CompilerParams(
            vmem_limit_bytes=48 * 2**20, dimension_semantics=("arbitrary",)
        ),
        cost_estimate=pl.CostEstimate(
            flops=6 * 10**9, bytes_accessed=16 * 10**6, transcendentals=4 * 10**6
        ),
        name="pairs",
    )(pairs, counts, queries, upstream, gate, k0, v0, kvm1, kvp1, km2, vm2, kp2, vp2)


def moved(shard, by):
    count = lax.axis_size(TIME)
    return lax.ppermute(shard, TIME, [(i, (i + by) % count) for i in range(count)])


def summed(part, axis, masks):
    count = lax.axis_size(axis)
    a, b, c = (
        lax.ppermute(part, axis, [(i, i ^ mask) for i in range(count)]) for mask in masks
    )
    return (part + a) + (b + c)


def shards(video_query, audio_key, audio_value, cross_gate, grad_out, pair_blocks, pair_count):
    width = cross_gate.shape[0]
    key = audio_key[0]
    value = audio_value[0]
    km2 = moved(key, 2)
    vp2 = moved(value, -2)
    both = jnp.stack([key, value])
    kvm1 = moved(both, 1)
    kvp1 = moved(both, -1)
    kp2 = moved(km2, -4)
    vm2 = moved(vp2, 4)
    out, qgrad, gate_part, own, dm1, dp1, dkm2, dvm2, dkp2, dvp2 = attend_pairs(
        pair_blocks, pair_count, video_query, grad_out, cross_gate.reshape(1, width),
        audio_key, audio_value, kvm1, kvp1, km2, vm2, kp2, vp2,
    )
    after = moved(dm1, -1)
    before = moved(dp1, 1)
    kfar = moved(dkp2, 4)
    vfar = moved(dvm2, -4)
    gate_part, kfar, vfar = lax.optimization_barrier((gate_part, kfar, vfar))
    gate_part = summed(gate_part, "clip", (1, 2, 3))
    gate_part, after, before, kfar, vfar = lax.optimization_barrier(
        (gate_part, after, before, kfar, vfar)
    )
    kfar = moved((dkm2.astype(F32) + kfar.astype(F32)).astype(BF16), -2)
    vfar = moved((dvp2.astype(F32) + vfar.astype(F32)).astype(BF16), 2)
    gate_part = summed(gate_part, "vid", (1, 2, 3))
    gate_part = summed(gate_part, "vid", (4, 8, 12))
    gate_part = summed(gate_part, "aud", (1, 2, 3))
    near = own + after.astype(F32) + before.astype(F32)
    key_grad = (near[0] + kfar.astype(F32)).astype(BF16)[None]
    value_grad = (near[1] + vfar.astype(F32)).astype(BF16)[None]
    return (out, qgrad, key_grad, value_grad, gate_part.reshape(width))


def solution(mesh):
    tokens = P("clip", TIME, None)
    in_specs = (tokens, tokens, tokens, P(), tokens, tokens, P("clip", TIME))
    out_specs = (tokens, tokens, tokens, tokens, P())
    return jax.shard_map(shards, mesh=mesh, in_specs=in_specs, out_specs=out_specs, check_vma=False)
```

```python
import math

import jax
import jax.numpy as jnp
from jax import lax
from jax.experimental import pallas as pl
from jax.experimental.pallas import tpu as pltpu
from jax.sharding import PartitionSpec as P

HEADS = 12
HEAD_DIM = 128
BLOCK = 128
REACH = 2
MAXP = 4
WINDOW = 2 * REACH + 1
GROUP = 2
LANES = 256
ROWS = 64
SCALE = HEAD_DIM**-0.5
LOG2E = math.log2(math.e)
F32 = jnp.float32
BF16 = jnp.bfloat16
TIME = ("vid", "aud")


def nn(a, b):
    return lax.dot_general(a, b, (((1,), (0,)), ((), ())), preferred_element_type=F32)


def nt(a, b):
    return lax.dot_general(a, b, (((1,), (1,)), ((), ())), preferred_element_type=F32)


def tn(a, b):
    return lax.dot_general(a, b, (((0,), (0,)), ((), ())), preferred_element_type=F32)


def weigh(pairs, counts, slot, block):
    times = jnp.int32(0)
    for s in range(MAXP):
        named = pairs[0, block, s] - pairs[0, block, 0] + REACH == slot
        times = times + jnp.where(jnp.logical_and(named, s < counts[0, block]), 1, 0)
    several = jnp.where(times == 2, 1.0, jnp.where(times == 3, math.log2(3.0), 2.0))
    return jnp.where(times == 0, -1e30, jnp.where(times == 1, 0.0, several))


def pair_kernel(pairs, counts, q_ref, up_ref, gate_ref, *refs):
    k_refs, v_refs = refs[:WINDOW], refs[WINDOW : 2 * WINDOW]
    out_ref, qgrad_ref, gpart_ref = refs[2 * WINDOW : 2 * WINDOW + 3]
    grad_refs = refs[2 * WINDOW + 3 : 3 * WINDOW + 3]
    bias_ref, expo_ref = refs[3 * WINDOW + 3 :]

    def hand_out(grads, which, cols):
        for w, ref in enumerate(grad_refs):
            ref[which, :, cols] = grads[w * BLOCK : (w + 1) * BLOCK].astype(ref.dtype)

    @pl.when(pl.program_id(0) == 0)
    def _():
        for slot in range(WINDOW):
            for block in range(4):
                bias_ref[slot : slot + 1, block * BLOCK : (block + 1) * BLOCK] = jnp.full(
                    (1, BLOCK), weigh(pairs, counts, slot, block), F32
                )

    fold = SCALE * LOG2E
    vrows = q_ref.shape[1]
    for head in range(GROUP):
        cols = slice(head * HEAD_DIM, (head + 1) * HEAD_DIM)

        keys = jnp.concatenate([r[:, cols] for r in k_refs], axis=0)
        values = jnp.concatenate([r[:, cols] for r in v_refs], axis=0)
        gate = gate_ref[:, cols]
        dattend_t = (up_ref[0, :, cols].astype(F32) * gate).astype(BF16).T
        scaled = []
        inverses = []
        for at in range(0, vrows, LANES):
            lanes = slice(at, at + LANES)
            scores = nt(keys, q_ref[0, lanes, cols])
            bias = [bias_ref[slot : slot + 1, lanes] for slot in range(WINDOW)]
            top = None
            for slot in range(WINDOW):
                part = scores[slot * BLOCK : (slot + 1) * BLOCK]
                part = jnp.max(part, axis=0, keepdims=True) * fold + bias[slot]
                top = part if top is None else jnp.maximum(top, part)
            total = jnp.zeros((8, LANES), F32)
            for slot in range(WINDOW):
                shift = jnp.broadcast_to(bias[slot] - top, (ROWS, LANES))
                for row in range(slot * BLOCK, (slot + 1) * BLOCK, ROWS):
                    expo = jnp.exp2(scores[row : row + ROWS] * fold + shift)
                    for i in range(0, ROWS, 8):
                        total = total + expo[i : i + 8]
                    expo_ref[head, row : row + ROWS, lanes] = expo.astype(BF16)
            inverse = 1.0 / jnp.sum(total, axis=0, keepdims=True)
            inverses.append(inverse)
            scaled.append((dattend_t[:, lanes].astype(F32) * inverse).astype(BF16))
        scaled = jnp.concatenate(scaled, axis=1)
        attend_t = tn(values, expo_ref[head]) * jnp.concatenate(inverses, axis=1)
        attend = attend_t.T
        out_ref[0, :, cols] = (attend * gate).astype(BF16)
        gpart_ref[:, cols] = jnp.sum(
            attend * up_ref[0, :, cols].astype(F32), axis=0, keepdims=True
        )
        hand_out(nt(expo_ref[head], scaled), 1, cols)
        dscore = []
        for at in range(0, vrows, LANES):
            lanes = slice(at, at + LANES)
            dat = scaled[:, lanes]
            delta = jnp.sum(attend_t[:, lanes] * dat.astype(F32), axis=0, keepdims=True)
            dprob = nn(values, dat)
            dscore.append(
                jnp.concatenate(
                    [
                        (
                            expo_ref[head, row : row + ROWS, lanes].astype(F32)
                            * (dprob[row : row + ROWS] - delta)
                        ).astype(BF16)
                        for row in range(0, WINDOW * BLOCK, ROWS)
                    ],
                    axis=0,
                )
            )
        dscore = jnp.concatenate(dscore, axis=1)
        qgrad_ref[0, :, cols] = (tn(keys, dscore) * SCALE).astype(BF16).T
        hand_out(nn(dscore, q_ref[0, :, cols]) * SCALE, 0, cols)


def attend_pairs(pairs, counts, queries, upstream, gate, keys, values):
    vrows, width = queries.shape[1:]
    cols = GROUP * HEAD_DIM
    smem = pl.BlockSpec(memory_space=pltpu.SMEM)
    video = pl.BlockSpec((1, vrows, cols), lambda h: (0, 0, h))
    one = pl.BlockSpec((BLOCK, cols), lambda h: (0, h))
    both = pl.BlockSpec((2, BLOCK, cols), lambda h: (0, 0, h))
    row = pl.BlockSpec((1, cols), lambda h: (0, h))
    shape = jax.ShapeDtypeStruct
    return pl.pallas_call(
        pair_kernel,
        grid=(HEADS // GROUP,),
        in_specs=[smem, smem, video, video, row] + [one] * (2 * WINDOW),
        out_specs=[video, video, row] + [both] * WINDOW,
        out_shape=[
            shape((1, vrows, width), BF16),
            shape((1, vrows, width), BF16),
            shape((1, width), F32),
        ]
        + [shape((2, BLOCK, width), F32 if w == REACH else BF16) for w in range(WINDOW)],
        scratch_shapes=[
            pltpu.VMEM((8, vrows), F32),
            pltpu.VMEM((GROUP, WINDOW * BLOCK, vrows), BF16),
        ],
        compiler_params=pltpu.CompilerParams(
            vmem_limit_bytes=60 * 2**20, dimension_semantics=("arbitrary",)
        ),
        cost_estimate=pl.CostEstimate(
            flops=6 * 10**9, bytes_accessed=16 * 10**6, transcendentals=4 * 10**6
        ),
        name="pairs",
    )(pairs, counts, queries, upstream, gate, *keys, *values)


def moved(shard, by):
    count = lax.axis_size(TIME)
    return lax.ppermute(shard, TIME, [(i, (i + by) % count) for i in range(count)])


def joined(part, arrived):
    return (part.astype(F32) + arrived.astype(F32)).astype(BF16)


def summed(part, axis, masks):
    count = lax.axis_size(axis)
    a, b, c = (
        lax.ppermute(part, axis, [(i, i ^ mask) for i in range(count)]) for mask in masks
    )
    return (part + a) + (b + c)


def shards(video_query, audio_key, audio_value, cross_gate, grad_out, pair_blocks, pair_count):
    width = cross_gate.shape[0]
    key, value = audio_key[0], audio_value[0]
    km1, kp1 = moved(key, 1), moved(key, -1)
    vm1, vp1 = moved(value, 1), moved(value, -1)
    km2, kp2 = moved(km1, 1), moved(kp1, -1)
    vm2, vp2 = moved(vm1, 1), moved(vp1, -1)
    out, qgrad, gate_part, m2, m1, own, p1, p2 = attend_pairs(
        pair_blocks, pair_count, video_query, grad_out, cross_gate.reshape(1, width),
        (km2, km1, key, kp1, kp2), (vm2, vm1, value, vp1, vp2),
    )
    m2, p2 = moved(m2, -1), moved(p2, 1)
    gate_part = summed(gate_part, "clip", (1, 2, 3))
    gate_part = summed(gate_part, "vid", (1, 2, 3))
    gate_part, m2, p2 = lax.optimization_barrier((gate_part, m2, p2))
    m1, p1 = moved(joined(m1, m2), -1), moved(joined(p1, p2), 1)
    gate_part = summed(gate_part, "vid", (4, 8, 12))
    gate_part = summed(gate_part, "aud", (1, 2, 3))
    grads = (own + m1.astype(F32) + p1.astype(F32)).astype(BF16)
    return (out, qgrad, grads[:1], grads[1:], gate_part.reshape(width))


def solution(mesh):
    tokens = P("clip", TIME, None)
    in_specs = (tokens, tokens, tokens, P(), tokens, tokens, P("clip", TIME))
    out_specs = (tokens, tokens, tokens, tokens, P())
    return jax.shard_map(shards, mesh=mesh, in_specs=in_specs, out_specs=out_specs, check_vma=False)
```

```python
import math

import jax
import jax.numpy as jnp
from jax import lax
from jax.experimental import pallas as pl
from jax.experimental.pallas import tpu as pltpu
from jax.sharding import PartitionSpec as P

HEADS = 12
HEAD_DIM = 128
BLOCK = 128
REACH = 2
MAXP = 4
WINDOW = 2 * REACH + 1
GROUP = 4
LAG = 2
LANES = 256
ROWS = 64
SCALE = HEAD_DIM**-0.5
LOG2E = math.log2(math.e)
F32 = jnp.float32
BF16 = jnp.bfloat16
TIME = ("vid", "aud")


def nn(a, b):
    return lax.dot_general(a, b, (((1,), (0,)), ((), ())), preferred_element_type=F32)


def nt(a, b):
    return lax.dot_general(a, b, (((1,), (1,)), ((), ())), preferred_element_type=F32)


def tn(a, b):
    return lax.dot_general(a, b, (((0,), (0,)), ((), ())), preferred_element_type=F32)


def weigh(pairs, counts, slot, block):
    times = jnp.int32(0)
    for s in range(MAXP):
        named = pairs[0, block, s] - pairs[0, block, 0] + REACH == slot
        times = times + jnp.where(jnp.logical_and(named, s < counts[0, block]), 1, 0)
    several = jnp.where(times == 2, 1.0, jnp.where(times == 3, math.log2(3.0), 2.0))
    return jnp.where(times == 0, -1e30, jnp.where(times == 1, 0.0, several))


def pair_kernel(pairs, counts, q_ref, up_ref, gate_ref, *refs):
    k_refs, v_refs = refs[:WINDOW], refs[WINDOW : 2 * WINDOW]
    out_ref, qgrad_ref, gpart_ref = refs[2 * WINDOW : 2 * WINDOW + 3]
    grad_refs = refs[2 * WINDOW + 3 : 3 * WINDOW + 3]
    bias_ref, expo_ref = refs[3 * WINDOW + 3 :]

    def hand_out(grads, which, cols):
        for w, ref in enumerate(grad_refs):
            ref[which, :, cols] = grads[w * BLOCK : (w + 1) * BLOCK].astype(ref.dtype)

    @pl.when(pl.program_id(0) == 0)
    def _():
        for slot in range(WINDOW):
            for block in range(4):
                bias_ref[slot : slot + 1, block * BLOCK : (block + 1) * BLOCK] = jnp.full(
                    (1, BLOCK), weigh(pairs, counts, slot, block), F32
                )

    fold = SCALE * LOG2E
    vrows = q_ref.shape[1]
    def work(head):
        cols = slice(head * HEAD_DIM, (head + 1) * HEAD_DIM)
        keys = jnp.concatenate([r[:, cols] for r in k_refs], axis=0)
        values = jnp.concatenate([r[:, cols] for r in v_refs], axis=0)
        gate = gate_ref[:, cols]
        dattend_t = (up_ref[0, :, cols].astype(F32) * gate).astype(BF16).T
        chunks = [slice(at, at + LANES) for at in range(0, vrows, LANES)]
        scaled = []
        inverses = []
        for lanes in chunks:
            scores = nt(keys, q_ref[0, lanes, cols])
            yield
            bias = [bias_ref[slot : slot + 1, lanes] for slot in range(WINDOW)]
            top = None
            for slot in range(WINDOW):
                part = scores[slot * BLOCK : (slot + 1) * BLOCK]
                part = jnp.max(part, axis=0, keepdims=True) * fold + bias[slot]
                top = part if top is None else jnp.maximum(top, part)
            total = jnp.zeros((8, LANES), F32)
            for slot in range(WINDOW):
                shift = jnp.broadcast_to(bias[slot] - top, (ROWS, LANES))
                for row in range(slot * BLOCK, (slot + 1) * BLOCK, ROWS):
                    expo = jnp.exp2(scores[row : row + ROWS] * fold + shift)
                    for i in range(0, ROWS, 8):
                        total = total + expo[i : i + 8]
                    expo_ref[head, row : row + ROWS, lanes] = expo.astype(BF16)
            inverse = 1.0 / jnp.sum(total, axis=0, keepdims=True)
            inverses.append(inverse)
            scaled.append((dattend_t[:, lanes].astype(F32) * inverse).astype(BF16))
            yield
        attend_t = tn(values, expo_ref[head]) * jnp.concatenate(inverses, axis=1)
        yield
        hand_out(nt(expo_ref[head], jnp.concatenate(scaled, axis=1)), 1, cols)
        yield
        dscore = []
        for lanes, dat in zip(chunks, scaled):
            delta = jnp.sum(attend_t[:, lanes] * dat.astype(F32), axis=0, keepdims=True)
            dprob = nn(values, dat)
            yield
            dscore.append(
                jnp.concatenate(
                    [
                        (
                            expo_ref[head, row : row + ROWS, lanes].astype(F32)
                            * (dprob[row : row + ROWS] - delta)
                        ).astype(BF16)
                        for row in range(0, WINDOW * BLOCK, ROWS)
                    ],
                    axis=0,
                )
            )
            yield
        dscore = jnp.concatenate(dscore, axis=1)
        attend = attend_t.T
        out_ref[0, :, cols] = (attend * gate).astype(BF16)
        gpart_ref[:, cols] = jnp.sum(
            attend * up_ref[0, :, cols].astype(F32), axis=0, keepdims=True
        )
        yield
        qgrad_ref[0, :, cols] = (tn(keys, dscore) * SCALE).astype(BF16).T
        yield
        hand_out(nn(dscore, q_ref[0, :, cols]) * SCALE, 0, cols)

    heads = [work(head) for head in range(GROUP)]
    turn = 0
    while any(h is not None for h in heads):
        for i, h in enumerate(heads):
            if h is not None and turn >= i * LAG and next(h, 0) == 0:
                heads[i] = None
        turn += 1


def attend_pairs(pairs, counts, queries, upstream, gate, keys, values):
    vrows, width = queries.shape[1:]
    cols = GROUP * HEAD_DIM
    smem = pl.BlockSpec(memory_space=pltpu.SMEM)
    video = pl.BlockSpec((1, vrows, cols), lambda h: (0, 0, h))
    one = pl.BlockSpec((BLOCK, cols), lambda h: (0, h))
    both = pl.BlockSpec((2, BLOCK, cols), lambda h: (0, 0, h))
    row = pl.BlockSpec((1, cols), lambda h: (0, h))
    shape = jax.ShapeDtypeStruct
    return pl.pallas_call(
        pair_kernel,
        grid=(HEADS // GROUP,),
        in_specs=[smem, smem, video, video, row] + [one] * (2 * WINDOW),
        out_specs=[video, video, row] + [both] * WINDOW,
        out_shape=[
            shape((1, vrows, width), BF16),
            shape((1, vrows, width), BF16),
            shape((1, width), F32),
        ]
        + [shape((2, BLOCK, width), F32 if w == REACH else BF16) for w in range(WINDOW)],
        scratch_shapes=[
            pltpu.VMEM((8, vrows), F32),
            pltpu.VMEM((GROUP, WINDOW * BLOCK, vrows), BF16),
        ],
        compiler_params=pltpu.CompilerParams(
            vmem_limit_bytes=60 * 2**20, dimension_semantics=("arbitrary",)
        ),
        cost_estimate=pl.CostEstimate(
            flops=6 * 10**9, bytes_accessed=16 * 10**6, transcendentals=4 * 10**6
        ),
        name="pairs",
    )(pairs, counts, queries, upstream, gate, *keys, *values)


def moved(shard, by):
    count = lax.axis_size(TIME)
    return lax.ppermute(shard, TIME, [(i, (i + by) % count) for i in range(count)])


def joined(part, arrived):
    return (part.astype(F32) + arrived.astype(F32)).astype(BF16)


def summed(part, axis, masks):
    count = lax.axis_size(axis)
    a, b, c = (
        lax.ppermute(part, axis, [(i, i ^ mask) for i in range(count)]) for mask in masks
    )
    return (part + a) + (b + c)


def shards(video_query, audio_key, audio_value, cross_gate, grad_out, pair_blocks, pair_count):
    width = cross_gate.shape[0]
    key, value = audio_key[0], audio_value[0]
    km1, kp1 = moved(key, 1), moved(key, -1)
    vm1, vp1 = moved(value, 1), moved(value, -1)
    km2, kp2 = moved(km1, 1), moved(kp1, -1)
    vm2, vp2 = moved(vm1, 1), moved(vp1, -1)
    out, qgrad, gate_part, m2, m1, own, p1, p2 = attend_pairs(
        pair_blocks, pair_count, video_query, grad_out, cross_gate.reshape(1, width),
        (km2, km1, key, kp1, kp2), (vm2, vm1, value, vp1, vp2),
    )
    m2, p2 = moved(m2, -1), moved(p2, 1)
    gate_part = summed(gate_part, "clip", (1, 2, 3))
    gate_part = summed(gate_part, "vid", (4, 8, 12))
    gate_part, m2, p2 = lax.optimization_barrier((gate_part, m2, p2))
    m1, p1 = moved(joined(m1, m2), -1), moved(joined(p1, p2), 1)
    gate_part = summed(gate_part, "vid", (1, 2, 3))
    gate_part = summed(gate_part, "aud", (1, 2, 3))
    grads = (own + m1.astype(F32) + p1.astype(F32)).astype(BF16)
    return (out, qgrad, grads[:1], grads[1:], gate_part.reshape(width))


def solution(mesh):
    tokens = P("clip", TIME, None)
    in_specs = (tokens, tokens, tokens, P(), tokens, tokens, P("clip", TIME))
    out_specs = (tokens, tokens, tokens, tokens, P())
    return jax.shard_map(shards, mesh=mesh, in_specs=in_specs, out_specs=out_specs, check_vma=False)
```

```python
import math

import jax
import jax.numpy as jnp
from jax import lax
from jax.experimental import pallas as pl
from jax.experimental.pallas import tpu as pltpu
from jax.sharding import PartitionSpec as P

HEADS = 12
HEAD_DIM = 128
BLOCK = 128
REACH = 2
MAXP = 4
WINDOW = 2 * REACH + 1
GROUP = 4
LAG = 2
LANES = 256
ROWS = 64
SCALE = HEAD_DIM**-0.5
LOG2E = math.log2(math.e)
F32 = jnp.float32
BF16 = jnp.bfloat16
TIME = ("vid", "aud")


def nn(a, b):
    return lax.dot_general(a, b, (((1,), (0,)), ((), ())), preferred_element_type=F32)


def nt(a, b):
    return lax.dot_general(a, b, (((1,), (1,)), ((), ())), preferred_element_type=F32)


def tn(a, b):
    return lax.dot_general(a, b, (((0,), (0,)), ((), ())), preferred_element_type=F32)


def weigh(pairs, counts, slot, block):
    times = jnp.int32(0)
    for s in range(MAXP):
        named = pairs[0, block, s] - pairs[0, block, 0] + REACH == slot
        times = times + jnp.where(jnp.logical_and(named, s < counts[0, block]), 1, 0)
    several = jnp.where(times == 2, 1.0, jnp.where(times == 3, math.log2(3.0), 2.0))
    return jnp.where(times == 0, -1e30, jnp.where(times == 1, 0.0, several))


def pair_kernel(pairs, counts, q_ref, up_ref, gate_ref, *refs):
    k_refs, v_refs = refs[:WINDOW], refs[WINDOW : 2 * WINDOW]
    out_ref, qgrad_ref, gpart_ref = refs[2 * WINDOW : 2 * WINDOW + 3]
    grad_refs = refs[2 * WINDOW + 3 : 3 * WINDOW + 3]
    bias_ref, expo_ref = refs[3 * WINDOW + 3 :]

    def hand_out(grads, which, cols):
        for w, ref in enumerate(grad_refs):
            ref[which, :, cols] = grads[w * BLOCK : (w + 1) * BLOCK].astype(ref.dtype)

    @pl.when(pl.program_id(0) == 0)
    def _():
        for slot in range(WINDOW):
            for block in range(4):
                bias_ref[slot : slot + 1, block * BLOCK : (block + 1) * BLOCK] = jnp.full(
                    (1, BLOCK), weigh(pairs, counts, slot, block), F32
                )

    fold = SCALE * LOG2E
    vrows = q_ref.shape[1]
    def work(head):
        cols = slice(head * HEAD_DIM, (head + 1) * HEAD_DIM)
        keys = jnp.concatenate([r[:, cols] for r in k_refs], axis=0)
        values = jnp.concatenate([r[:, cols] for r in v_refs], axis=0)
        gate = gate_ref[:, cols]
        dattend_t = (up_ref[0, :, cols].astype(F32) * gate).astype(BF16).T
        chunks = [slice(at, at + LANES) for at in range(0, vrows, LANES)]
        scaled = []
        inverses = []
        for lanes in chunks:
            scores = nt(keys, q_ref[0, lanes, cols])
            yield
            bias = [bias_ref[slot : slot + 1, lanes] for slot in range(WINDOW)]
            top = None
            for slot in range(WINDOW):
                part = scores[slot * BLOCK : (slot + 1) * BLOCK]
                part = jnp.max(part, axis=0, keepdims=True) * fold + bias[slot]
                top = part if top is None else jnp.maximum(top, part)
            total = jnp.zeros((8, LANES), F32)
            for slot in range(WINDOW):
                shift = jnp.broadcast_to(bias[slot] - top, (ROWS, LANES))
                for row in range(slot * BLOCK, (slot + 1) * BLOCK, ROWS):
                    expo = jnp.exp2(scores[row : row + ROWS] * fold + shift)
                    for i in range(0, ROWS, 8):
                        total = total + expo[i : i + 8]
                    expo_ref[head, row : row + ROWS, lanes] = expo.astype(BF16)
            inverse = 1.0 / jnp.sum(total, axis=0, keepdims=True)
            inverses.append(inverse)
            scaled.append((dattend_t[:, lanes].astype(F32) * inverse).astype(BF16))
            yield
        attend_t = tn(values, expo_ref[head]) * jnp.concatenate(inverses, axis=1)
        yield
        hand_out(nt(expo_ref[head], jnp.concatenate(scaled, axis=1)), 1, cols)
        yield
        dscore = []
        for lanes, dat in zip(chunks, scaled):
            delta = jnp.sum(attend_t[:, lanes] * dat.astype(F32), axis=0, keepdims=True)
            dprob = nn(values, dat)
            yield
            dscore.append(
                jnp.concatenate(
                    [
                        (
                            expo_ref[head, row : row + ROWS, lanes].astype(F32)
                            * (dprob[row : row + ROWS] - delta)
                        ).astype(BF16)
                        for row in range(0, WINDOW * BLOCK, ROWS)
                    ],
                    axis=0,
                )
            )
            yield
        dscore = jnp.concatenate(dscore, axis=1)
        attend = attend_t.T
        out_ref[0, :, cols] = (attend * gate).astype(BF16)
        gpart_ref[:, cols] = jnp.sum(
            attend * up_ref[0, :, cols].astype(F32), axis=0, keepdims=True
        )
        yield
        qgrad_ref[0, :, cols] = (tn(keys, dscore) * SCALE).astype(BF16).T
        yield
        hand_out(nn(dscore, q_ref[0, :, cols]) * SCALE, 0, cols)

    heads = [work(head) for head in range(GROUP)]
    turn = 0
    while any(h is not None for h in heads):
        for i, h in enumerate(heads):
            if h is not None and turn >= i * LAG and next(h, 0) == 0:
                heads[i] = None
        turn += 1


def attend_pairs(pairs, counts, queries, upstream, gate, keys, values):
    vrows, width = queries.shape[1:]
    cols = GROUP * HEAD_DIM
    smem = pl.BlockSpec(memory_space=pltpu.SMEM)
    video = pl.BlockSpec((1, vrows, cols), lambda h: (0, 0, h))
    one = pl.BlockSpec((BLOCK, cols), lambda h: (0, h))
    both = pl.BlockSpec((2, BLOCK, cols), lambda h: (0, 0, h))
    row = pl.BlockSpec((1, cols), lambda h: (0, h))
    shape = jax.ShapeDtypeStruct
    return pl.pallas_call(
        pair_kernel,
        grid=(HEADS // GROUP,),
        in_specs=[smem, smem, video, video, row] + [one] * (2 * WINDOW),
        out_specs=[video, video, row] + [both] * WINDOW,
        out_shape=[
            shape((1, vrows, width), BF16),
            shape((1, vrows, width), BF16),
            shape((1, width), F32),
        ]
        + [shape((2, BLOCK, width), F32 if w == REACH else BF16) for w in range(WINDOW)],
        scratch_shapes=[
            pltpu.VMEM((8, vrows), F32),
            pltpu.VMEM((GROUP, WINDOW * BLOCK, vrows), BF16),
        ],
        compiler_params=pltpu.CompilerParams(
            vmem_limit_bytes=60 * 2**20, dimension_semantics=("arbitrary",)
        ),
        cost_estimate=pl.CostEstimate(
            flops=6 * 10**9, bytes_accessed=16 * 10**6, transcendentals=4 * 10**6
        ),
        name="pairs",
    )(pairs, counts, queries, upstream, gate, *keys, *values)


def moved(shard, by):
    count = lax.axis_size(TIME)
    return lax.ppermute(shard, TIME, [(i, (i + by) % count) for i in range(count)])


def joined(part, arrived):
    return (part.astype(F32) + arrived.astype(F32)).astype(BF16)


def summed(part, axis, masks):
    count = lax.axis_size(axis)
    a, b, c = (
        lax.ppermute(part, axis, [(i, i ^ mask) for i in range(count)]) for mask in masks
    )
    return (part + a) + (b + c)


def paired(part, axis, mask):
    count = lax.axis_size(axis)
    return part + lax.ppermute(part, axis, [(i, i ^ mask) for i in range(count)])


def shards(video_query, audio_key, audio_value, cross_gate, grad_out, pair_blocks, pair_count):
    width = cross_gate.shape[0]
    key, value = audio_key[0], audio_value[0]
    km1, kp1 = moved(key, 1), moved(key, -1)
    vm1, vp1 = moved(value, 1), moved(value, -1)
    km2, kp2 = moved(km1, 1), moved(kp1, -1)
    vm2, vp2 = moved(vm1, 1), moved(vp1, -1)
    out, qgrad, gate_part, m2, m1, own, p1, p2 = attend_pairs(
        pair_blocks, pair_count, video_query, grad_out, cross_gate.reshape(1, width),
        (km2, km1, key, kp1, kp2), (vm2, vm1, value, vp1, vp2),
    )
    m2, p2 = moved(m2, -1), moved(p2, 1)
    gate_part = paired(gate_part, "clip", 1)
    gate_part = summed(gate_part, "vid", (4, 8, 12))
    gate_part, m2, p2 = lax.optimization_barrier((gate_part, m2, p2))
    m1, p1 = moved(joined(m1, m2), -1), moved(joined(p1, p2), 1)
    gate_part = paired(gate_part, "clip", 2)
    gate_part = summed(gate_part, "vid", (1, 2, 3))
    gate_part = summed(gate_part, "aud", (1, 2, 3))
    grads = (own + m1.astype(F32) + p1.astype(F32)).astype(BF16)
    return (out, qgrad, grads[:1], grads[1:], gate_part.reshape(width))


def solution(mesh):
    tokens = P("clip", TIME, None)
    in_specs = (tokens, tokens, tokens, P(), tokens, tokens, P("clip", TIME))
    out_specs = (tokens, tokens, tokens, tokens, P())
    return jax.shard_map(shards, mesh=mesh, in_specs=in_specs, out_specs=out_specs, check_vma=False)
```

```python
import math

import jax
import jax.numpy as jnp
from jax import lax
from jax.experimental import pallas as pl
from jax.experimental.pallas import tpu as pltpu
from jax.sharding import PartitionSpec as P

HEADS = 12
HEAD_DIM = 128
BLOCK = 128
REACH = 2
MAXP = 4
WINDOW = 2 * REACH + 1
GROUP = 4
LAG = 2
LANES = 256
ROWS = 64
SCALE = HEAD_DIM**-0.5
LOG2E = math.log2(math.e)
F32 = jnp.float32
BF16 = jnp.bfloat16
TIME = ("vid", "aud")


def nn(a, b):
    return lax.dot_general(a, b, (((1,), (0,)), ((), ())), preferred_element_type=F32)


def nt(a, b):
    return lax.dot_general(a, b, (((1,), (1,)), ((), ())), preferred_element_type=F32)


def tn(a, b):
    return lax.dot_general(a, b, (((0,), (0,)), ((), ())), preferred_element_type=F32)


def weigh(pairs, counts, slot, block):
    times = jnp.int32(0)
    for s in range(MAXP):
        named = pairs[0, block, s] - pairs[0, block, 0] + REACH == slot
        times = times + jnp.where(jnp.logical_and(named, s < counts[0, block]), 1, 0)
    several = jnp.where(times == 2, 1.0, jnp.where(times == 3, math.log2(3.0), 2.0))
    return jnp.where(times == 0, -1e30, jnp.where(times == 1, 0.0, several))


def pair_kernel(pairs, counts, q_ref, up_ref, gate_ref, *refs):
    k_refs, v_refs = refs[:WINDOW], refs[WINDOW : 2 * WINDOW]
    out_ref, qgrad_ref, gpart_ref = refs[2 * WINDOW : 2 * WINDOW + 3]
    grad_refs = refs[2 * WINDOW + 3 : 3 * WINDOW + 3]
    bias_ref, expo_ref = refs[3 * WINDOW + 3 :]

    def hand_out(grads, which, cols):
        for w, ref in enumerate(grad_refs):
            ref[which, :, cols] = grads[w * BLOCK : (w + 1) * BLOCK].astype(ref.dtype)

    @pl.when(pl.program_id(0) == 0)
    def _():
        for slot in range(WINDOW):
            for block in range(4):
                bias_ref[slot : slot + 1, block * BLOCK : (block + 1) * BLOCK] = jnp.full(
                    (1, BLOCK), weigh(pairs, counts, slot, block), F32
                )

    fold = SCALE * LOG2E
    vrows = q_ref.shape[1]
    def work(head):
        cols = slice(head * HEAD_DIM, (head + 1) * HEAD_DIM)
        keys = jnp.concatenate([r[:, cols] for r in k_refs], axis=0)
        values = jnp.concatenate([r[:, cols] for r in v_refs], axis=0)
        gate = gate_ref[:, cols]
        dattend_t = (up_ref[0, :, cols].astype(F32) * gate).astype(BF16).T
        chunks = [slice(at, at + LANES) for at in range(0, vrows, LANES)]
        scaled = []
        inverses = []
        for lanes in chunks:
            scores = nt(keys, q_ref[0, lanes, cols])
            yield
            bias = [bias_ref[slot : slot + 1, lanes] for slot in range(WINDOW)]
            top = None
            for slot in range(WINDOW):
                part = scores[slot * BLOCK : (slot + 1) * BLOCK]
                part = jnp.max(part, axis=0, keepdims=True) * fold + bias[slot]
                top = part if top is None else jnp.maximum(top, part)
            total = jnp.zeros((8, LANES), F32)
            for slot in range(WINDOW):
                shift = jnp.broadcast_to(bias[slot] - top, (ROWS, LANES))
                for row in range(slot * BLOCK, (slot + 1) * BLOCK, ROWS):
                    expo = jnp.exp2(scores[row : row + ROWS] * fold + shift)
                    for i in range(0, ROWS, 8):
                        total = total + expo[i : i + 8]
                    expo_ref[head, row : row + ROWS, lanes] = expo.astype(BF16)
            inverse = 1.0 / jnp.sum(total, axis=0, keepdims=True)
            inverses.append(inverse)
            scaled.append((dattend_t[:, lanes].astype(F32) * inverse).astype(BF16))
            yield
        attend_t = tn(values, expo_ref[head]) * jnp.concatenate(inverses, axis=1)
        yield
        hand_out(nt(expo_ref[head], jnp.concatenate(scaled, axis=1)), 1, cols)
        yield
        dscore = []
        for lanes, dat in zip(chunks, scaled):
            delta = jnp.sum(attend_t[:, lanes] * dat.astype(F32), axis=0, keepdims=True)
            dprob = nn(values, dat)
            yield
            dscore.append(
                jnp.concatenate(
                    [
                        (
                            expo_ref[head, row : row + ROWS, lanes].astype(F32)
                            * (dprob[row : row + ROWS] - delta)
                        ).astype(BF16)
                        for row in range(0, WINDOW * BLOCK, ROWS)
                    ],
                    axis=0,
                )
            )
            yield
        dscore = jnp.concatenate(dscore, axis=1)
        attend = attend_t.T
        out_ref[0, :, cols] = (attend * gate).astype(BF16)
        gpart_ref[:, cols] = jnp.sum(
            attend * up_ref[0, :, cols].astype(F32), axis=0, keepdims=True
        )
        yield
        qgrad_ref[0, :, cols] = (tn(keys, dscore) * SCALE).astype(BF16).T
        yield
        hand_out(nn(dscore, q_ref[0, :, cols]) * SCALE, 0, cols)

    heads = [work(head) for head in range(GROUP)]
    turn = 0
    while any(h is not None for h in heads):
        for i, h in enumerate(heads):
            if h is not None and turn >= i * LAG and next(h, 0) == 0:
                heads[i] = None
        turn += 1


def attend_pairs(pairs, counts, queries, upstream, gate, keys, values):
    vrows, width = queries.shape[1:]
    cols = GROUP * HEAD_DIM
    smem = pl.BlockSpec(memory_space=pltpu.SMEM)
    video = pl.BlockSpec((1, vrows, cols), lambda h: (0, 0, h))
    one = pl.BlockSpec((BLOCK, cols), lambda h: (0, h))
    both = pl.BlockSpec((2, BLOCK, cols), lambda h: (0, 0, h))
    row = pl.BlockSpec((1, cols), lambda h: (0, h))
    shape = jax.ShapeDtypeStruct
    return pl.pallas_call(
        pair_kernel,
        grid=(HEADS // GROUP,),
        in_specs=[smem, smem, video, video, row] + [one] * (2 * WINDOW),
        out_specs=[video, video, row] + [both] * WINDOW,
        out_shape=[
            shape((1, vrows, width), BF16),
            shape((1, vrows, width), BF16),
            shape((1, width), F32),
        ]
        + [shape((2, BLOCK, width), F32 if w == REACH else BF16) for w in range(WINDOW)],
        scratch_shapes=[
            pltpu.VMEM((8, vrows), F32),
            pltpu.VMEM((GROUP, WINDOW * BLOCK, vrows), BF16),
        ],
        compiler_params=pltpu.CompilerParams(
            vmem_limit_bytes=64 * 2**20 - 2**18, dimension_semantics=("arbitrary",)
        ),
        cost_estimate=pl.CostEstimate(
            flops=6 * 10**9, bytes_accessed=16 * 10**6, transcendentals=4 * 10**6
        ),
        name="pairs",
    )(pairs, counts, queries, upstream, gate, *keys, *values)


def moved(shard, by):
    count = lax.axis_size(TIME)
    return lax.ppermute(shard, TIME, [(i, (i + by) % count) for i in range(count)])


def joined(part, arrived):
    return (part.astype(F32) + arrived.astype(F32)).astype(BF16)


def summed(part, axis, masks):
    count = lax.axis_size(axis)
    a, b, c = (
        lax.ppermute(part, axis, [(i, i ^ mask) for i in range(count)]) for mask in masks
    )
    return (part + a) + (b + c)


def paired(part, axis, mask):
    count = lax.axis_size(axis)
    return part + lax.ppermute(part, axis, [(i, i ^ mask) for i in range(count)])


def shards(video_query, audio_key, audio_value, cross_gate, grad_out, pair_blocks, pair_count):
    width = cross_gate.shape[0]
    key, value = audio_key[0], audio_value[0]
    km1, kp1 = moved(key, 1), moved(key, -1)
    vm1, vp1 = moved(value, 1), moved(value, -1)
    km2, kp2 = moved(km1, 1), moved(kp1, -1)
    vm2, vp2 = moved(vm1, 1), moved(vp1, -1)
    out, qgrad, gate_part, m2, m1, own, p1, p2 = attend_pairs(
        pair_blocks, pair_count, video_query, grad_out, cross_gate.reshape(1, width),
        (km2, km1, key, kp1, kp2), (vm2, vm1, value, vp1, vp2),
    )
    m2, p2 = moved(m2, -1), moved(p2, 1)
    gate_part = paired(gate_part, "clip", 1)
    gate_part = summed(gate_part, "vid", (4, 8, 12))
    gate_part, m2, p2 = lax.optimization_barrier((gate_part, m2, p2))
    m1, p1 = moved(joined(m1, m2), -1), moved(joined(p1, p2), 1)
    gate_part = paired(gate_part, "clip", 2)
    gate_part = summed(gate_part, "vid", (1, 2, 3))
    gate_part = summed(gate_part, "aud", (1, 2, 3))
    grads = (own + m1.astype(F32) + p1.astype(F32)).astype(BF16)
    return (out, qgrad, grads[:1], grads[1:], gate_part.reshape(width))


def solution(mesh):
    tokens = P("clip", TIME, None)
    in_specs = (tokens, tokens, tokens, P(), tokens, tokens, P("clip", TIME))
    out_specs = (tokens, tokens, tokens, tokens, P())
    return jax.shard_map(shards, mesh=mesh, in_specs=in_specs, out_specs=out_specs, check_vma=False)
```
